128 devices in a mesh: row: 16 (over z, x), col: 8 (over y, core).
Axes of the slice: x: 4, y: 4, z: 4, core: 2. Of those that a mesh axis runs over, the one named last changes fastest.
Arguments:
- coords: float32 [2048, 3, 512], P(('row', 'col')), may hold values from -1 to 258, as said below
- rhs: bfloat16 [2048, 16, 512], P(('row', 'col')), may hold values from -6 to 6
- near_pairs: int32 [8192, 2], P(('row', 'col')), may hold values from -1 to 128, as said below
- far_list: int32 [2048, 32], P(('row', 'col')), may hold values from 0 to 2047
- basis: bfloat16 [2048, 32, 512], P(('row', 'col')), may hold values from -0.25 to 0.25
- coupling: bfloat16 [2048, 32, 32, 32], P(('row', 'col')), may hold values from -1 to 1
Outputs:
- potential: float32 [2048, 16, 512], P(('row', 'col'))
The draws below stay inside these ranges and needn't reach their ends.
Inputs may be any that keep to these rules, and one draw needn't show every extreme that they name: `near_pairs`: column 0 of a live slot names a local cluster (0 to 15); column 1 is -1 for an empty slot or o * 16 + l with the neighbour offset o (0 to 8) pointing inside the device grid. The second cluster of a live pair is the first one or one of the eight clusters next to it in the grid of clusters (device row times 16 plus local index, device column). Live slots of a device come first; one device has all 64 slots live; empty slots hold 0 in column 0. `coords`: cluster g with grid cell (i, j) = ((g // 16) // 8 * 16 + g % 16, (g // 16) % 8) has its panels in the box [i - 0.5, i + 1.5] x [j - 0.5, j + 1.5] x [0, 0.2].
All inputs are finite; a program needn't handle non-finite values.
Results may differ from the reference program's by a relative error of at most 0.003.
Values may be sent and summed in bfloat16 or wider, within the bound.
A program may use at most 64 MiB of HBM per device.

```python
import jax
import jax.numpy as jnp
from jax import lax

P_SIZE = 512
R = 16
K = 32
FAR = 32
CL_DEV = 16
NP_DEV = 64
NC = 2048
N_ROW = 16
N_COL = 8


def draw_coords(key, part):
    key = jax.random.fold_in(key, 5)
    cluster = jnp.arange(NC, dtype=jnp.int32)
    device = cluster // CL_DEV
    local = cluster % CL_DEV
    grid_row = device // N_COL
    grid_col = device % N_COL
    sample = jax.random.uniform(key, (NC, 3, P_SIZE), jnp.float32)
    plane_x = sample[:, 0]
    plane_y = sample[:, 1]
    pos_x = (grid_row * CL_DEV + local).astype(jnp.float32)[:, None] - 0.5 + 2.0 * plane_x
    pos_y = grid_col.astype(jnp.float32)[:, None] - 0.5 + 2.0 * plane_y
    pos_z = 0.2 * sample[:, 2]
    return jnp.stack([pos_x, pos_y, pos_z], axis=1)


def draw_near_pairs(key, part):
    key = jax.random.fold_in(key, 11)
    devices = N_ROW * N_COL
    keys = jax.random.split(key, 7)
    device = jnp.arange(devices, dtype=jnp.int32)
    light = jax.random.randint(keys[0], (devices,), NP_DEV // 4, NP_DEV // 2 + 1)
    heavy = jax.random.randint(keys[1], (devices,), 0, 8) == 0
    counts = jnp.where(heavy, NP_DEV, light)
    counts = counts.at[jax.random.randint(keys[2], (), 0, devices)].set(NP_DEV)
    slot = jnp.arange(NP_DEV, dtype=jnp.int32)
    alive = slot[None, :] < counts[:, None]
    grid_row = (device // N_COL)[:, None]
    grid_col = (device % N_COL)[:, None]
    first = jax.random.randint(keys[6], (devices, NP_DEV), 0, CL_DEV)
    step_x = jax.random.randint(keys[3], (devices, NP_DEV), -1, 2)
    step_y = jax.random.randint(keys[4], (devices, NP_DEV), -1, 2)
    first = first.at[0, 0].set(CL_DEV - 1)
    step_x = step_x.at[0, 0].set(1)
    step_y = step_y.at[0, 0].set(1)
    target_x = jnp.clip(grid_row * CL_DEV + first + step_x, 0, N_ROW * CL_DEV - 1)
    target_y = jnp.clip(grid_col + step_y, 0, N_COL - 1)
    target_row = target_x // CL_DEV
    target_local = target_x % CL_DEV
    offset = (target_row - grid_row + 1) * 3 + (target_y - grid_col + 1)
    second = offset * CL_DEV + target_local
    second = jnp.where(alive, second, -1)
    first = jnp.where(alive, first, 0)
    return jnp.stack([first, second], axis=-1).reshape(devices * NP_DEV, 2).astype(jnp.int32)


def place_ends(result, stream_key, smallest, top_value):
    shape = result.shape
    index_at = [jax.random.randint(jax.random.fold_in(stream_key, axis), (), 0, shape[axis]) for axis in range(len(shape))]
    result = result.at[tuple(index_at)].set(smallest)
    longest = shape.index(max(shape))
    index_at[longest] = (index_at[longest] + 1) % shape[longest]
    return result.at[tuple(index_at)].set(top_value)


def levels(own_key, dims, pieces, least, top_value):
    def one(axis_at, blocks):
        draws = jax.random.uniform(jax.random.fold_in(jax.random.fold_in(own_key, 6), axis_at), (blocks,), jnp.float32, least / len(pieces), top_value / len(pieces))
        return jnp.repeat(jnp.exp(draws), dims[axis_at] // blocks).reshape((-1,) + (1,) * (len(dims) - axis_at - 1))

    factor_of = one(*pieces[0])
    for cut in pieces[1:]:
        factor_of = factor_of * one(*cut)
    return factor_of


def noise(key, extent, scale, limit, cuts=(), kind=jnp.bfloat16):
    gain = levels(key, extent, cuts, -0.22, 0.18) if cuts else 1.0
    values = jax.random.normal(key, extent, jnp.float32) * scale * gain
    return jnp.minimum(jnp.maximum(values, -limit), limit).astype(kind)


def setup_inputs(seed: int = 0) -> dict:
    seeds = jax.random.split(jax.random.key(seed), 7)
    coords = draw_coords(jax.random.fold_in(seeds[6], 71), 0)
    rhs = noise(seeds[1], (NC, R, P_SIZE), 1.0, 6.0, ((0, 128),))
    near_pairs = draw_near_pairs(jax.random.fold_in(seeds[6], 71), 0)
    far_list = place_ends(jax.random.randint(seeds[3], (NC, FAR), 0, NC), jax.random.fold_in(seeds[3], 1), 0, NC - 1).astype(jnp.int32)
    basis = noise(seeds[4], (NC, K, P_SIZE), P_SIZE ** -0.5, 0.25, ((0, 128),))
    coupling = noise(seeds[5], (NC, FAR, K, K), K ** -0.5, 1.0, ((0, 128),))
    return {"coords": coords, "rhs": rhs, "near_pairs": near_pairs, "far_list": far_list, "basis": basis, "coupling": coupling}


COUPLE = 0.0625
SOFTEN = 0.0025

def kernel_tile(first, second):
    delta_x = first[0][:, None] - second[0][None, :]
    delta_y = first[1][:, None] - second[1][None, :]
    delta_z = first[2][:, None] - second[2][None, :]
    squared = delta_x * delta_x + delta_y * delta_y + delta_z * delta_z
    return (COUPLE / jnp.sqrt(squared + SOFTEN)).astype(jnp.bfloat16)

def reference(coords, rhs, near_pairs, far_list, basis, coupling):
    total_slots = near_pairs.shape[0]
    slot = jnp.arange(total_slots, dtype=jnp.int32)
    device = slot // NP_DEV
    grid_row = device // N_COL
    grid_col = device % N_COL
    first = (device * CL_DEV + near_pairs[:, 0]).astype(jnp.int32)
    second_raw = near_pairs[:, 1]
    live = second_raw >= 0
    second_pos = jnp.maximum(second_raw, 0)
    offset = second_pos // CL_DEV
    other_dev = (grid_row + offset // 3 - 1) * N_COL + (grid_col + offset % 3 - 1)
    second = jnp.where(live, other_dev * CL_DEV + second_pos % CL_DEV, first).astype(jnp.int32)

    def pair_step(acc, item):
        left, right, alive = item
        tile = kernel_tile(coords[left], coords[right])
        forward = jnp.dot(rhs[right], tile.T, preferred_element_type=jnp.float32)
        backward = jnp.dot(rhs[left], tile, preferred_element_type=jnp.float32)
        acc = acc.at[left].add(jnp.where(alive, forward, jnp.zeros_like(forward)))
        mirror = alive & (left != right)
        acc = acc.at[right].add(jnp.where(mirror, backward, jnp.zeros_like(backward)))
        return (acc, None)
    near0 = jnp.zeros(rhs.shape, jnp.float32)
    near, _ = lax.scan(pair_step, near0, (first, second, live))
    coeffs = jnp.einsum('crp,ckp->crk', rhs.astype(jnp.float32), basis.astype(jnp.float32)).astype(jnp.bfloat16)

    def far_one(item):
        ids, coup, bas = item
        picked = coeffs[ids].astype(jnp.float32)
        inner = jnp.einsum('frk,fkl->rl', picked, coup.astype(jnp.float32)).astype(jnp.bfloat16)
        return jnp.dot(inner, bas, preferred_element_type=jnp.float32)
    far = lax.map(far_one, (far_list, coupling, basis))
    return near + far
```

```python
import functools

import jax
import jax.numpy as jnp
from jax import lax
from jax.experimental import pallas as pl
from jax.experimental.pallas import tpu as pltpu
from jax.sharding import PartitionSpec as P

MESH = pl.DeviceIdType.MESH
BF = jnp.bfloat16
F32 = jnp.float32
SOFTEN = 0.0025
GAIN = 256.0

NR, NC = 16, 8
CL, R, PS, K, FAR, NP = 16, 16, 512, 32, 32, 64
CHUNK = 64
NEIGHBOURS = [(0, -1), (0, 1), (-1, -1), (-1, 0), (-1, 1), (1, -1), (1, 0), (1, 1)]


def place(row, col):
    return (lax.rem(row + NR, NR), lax.rem(col + NC, NC))


def pair_ids(pairs, s):
    a = pairs[0, s]
    b = pairs[1, s]
    b = jnp.where(b < 0, 4 * CL + a, b)
    o = b // CL
    l = b % CL
    drow = o // 3 - 1
    wc = o % 3
    wr = jnp.clip(1 + drow * CL + l, 0, CL + 1)
    return a, wc, wr


def make_tile(s, tile, pairs, tables, wc_ref, row0, col0):
    a, wc, wr = pair_ids(pairs, s)
    x0 = (row0 * CL + a).astype(F32) + 0.5
    y0 = col0.astype(F32) + 0.5
    at = pl.ds(wr + 7, 1)
    bx = wc_ref[wc, 0, at, :] - x0
    by = wc_ref[wc, 1, at, :] - y0
    bz = wc_ref[wc, 2, at, :]
    nb = GAIN * (bx * bx + by * by + bz * bz + SOFTEN)
    bx, by, bz = (-2.0 * GAIN) * bx, (-2.0 * GAIN) * by, (-2.0 * GAIN) * bz
    bx, by, bz, nb = [jnp.broadcast_to(v, (8, PS)) for v in (bx, by, bz, nb)]
    for p in range(0, PS, 16):
        for q in range(0, PS, 128):
            ql = slice(q, q + 128)
            halves = []
            for h in (p, p + 8):
                ax, ay, az, na = [tables[a, i, h : h + 8, :] for i in range(4)]
                sq = (na + nb[:, ql]) + ax * bx[:, ql]
                sq = sq + (ay * by[:, ql] + az * bz[:, ql])
                halves.append(lax.rsqrt(sq))
            tile[p : p + 16, ql] = jnp.concatenate(halves, axis=0).astype(BF)


def use_tile(s, tile, pairs, wr_ref, f_ref, b_ref):
    a, wc, wr = pair_ids(pairs, s)
    left = wr_ref[1, a + 1]
    right = wr_ref[wc, wr]
    t = tile[...]
    rows = pl.ds(pl.multiple_of(s * R, R), R)
    f_ref[rows, :] = lax.dot_general(
        right, t, (((1,), (1,)), ((), ())), preferred_element_type=F32
    ).astype(BF)
    b_ref[rows, :] = jnp.dot(left, t, preferred_element_type=F32).astype(BF)


def one_hot(codes, first, count):
    rows = lax.broadcasted_iota(jnp.int32, (count, NP * R), 0) + first
    return jnp.where(rows == codes, 1.0, 0.0).astype(BF)


def slot_codes(pairs_v):
    a = pairs_v[0:1, :]
    b = pairs_v[1:2, :]
    alive = b >= 0
    b = jnp.maximum(b, 0)
    o = lax.shift_right_logical(b, 4)
    l = lax.bitwise_and(b, 15)
    down = jnp.where(o >= 6, 2, jnp.where(o >= 3, 1, 0))
    wc = o - 3 * down
    wr = (down - 1) * CL + l + 1
    same = jnp.logical_and(o == 4, l == a)
    fwd = jnp.where(alive, a, -1)
    bwd = jnp.where(jnp.logical_and(alive, jnp.logical_not(same)), wc * (CL + 2) + wr, -1)
    slot = lax.broadcasted_iota(jnp.int32, (NP, NP * R), 0)
    lane = lax.broadcasted_iota(jnp.int32, (NP, NP * R), 1)
    spread = jnp.where(lax.shift_right_logical(lane, 4) == slot, 1.0, 0.0).astype(BF)
    inner = lax.bitwise_and(lax.broadcasted_iota(jnp.int32, (1, NP * R), 1), 15)
    out = []
    for v in (fwd, bwd):
        v = jnp.broadcast_to(v, (8, NP)).astype(F32).astype(BF)
        v = jnp.dot(v, spread, preferred_element_type=F32)[0:1, :]
        out.append(v.astype(jnp.int32) * R + inner)
    return out


def body(
    pairs, far, pairs_v, coords, rhs, basis, coupling, out,
    own_c, wc_ref, wr_ref, bas, cpl, tables, every, tile0, tile1, f_ref, b_ref,
    send, back_c, back_r,
    loc_sem, hs_sem, hr_sem, g1s, g1r, g2s, g2r, g3s, g3r, bs_sem, br_sem,
):
    row = lax.axis_index("row")
    col = lax.axis_index("col")
    core = lax.rem(col, 2)
    cy = col // 2

    loads = [
        pltpu.make_async_copy(coords, own_c, loc_sem.at[0]),
        pltpu.make_async_copy(rhs, wr_ref.at[1, pl.ds(1, CL)], loc_sem.at[1]),
        pltpu.make_async_copy(basis, bas, loc_sem.at[2]),
        pltpu.make_async_copy(coupling, cpl, loc_sem.at[3]),
        pltpu.make_async_copy(coords, wc_ref.at[1, :, pl.ds(8, CL)], loc_sem.at[4]),
    ]
    for c in loads:
        c.start()

    barrier = pltpu.get_barrier_semaphore()
    partners = [place(row + dr, col + dc) for dr, dc in NEIGHBOURS if dc]
    partners += [place(row, col + 2 * k) for k in (1, 2, 3)]
    partners += [place(row + k, col) for k in range(1, NR)]
    for target in partners:
        pl.semaphore_signal(barrier, inc=1, device_id=target, device_id_type=MESH)
    pl.semaphore_wait(barrier, len(partners))

    def remote(src, dst, s, r, target):
        return pltpu.make_async_remote_copy(
            src_ref=src, dst_ref=dst, send_sem=s, recv_sem=r, device_id=target, device_id_type=MESH
        )

    halo = []
    for k, (dr, dc) in enumerate(NEIGHBOURS):
        target = place(row + dr, col + dc)
        if dr == 0:
            pieces = [
                (rhs, wr_ref.at[1 - dc, pl.ds(1, CL)]),
                (coords, wc_ref.at[1 - dc, :, pl.ds(8, CL)]),
            ]
        elif dr == 1:
            pieces = [
                (rhs.at[pl.ds(CL - 1, 1)], wr_ref.at[1 - dc, pl.ds(0, 1)]),
                (coords.at[:, pl.ds(CL - 8, 8)], wc_ref.at[1 - dc, :, pl.ds(0, 8)]),
            ]
        else:
            pieces = [
                (rhs.at[pl.ds(0, 1)], wr_ref.at[1 - dc, pl.ds(CL + 1, 1)]),
                (coords.at[:, pl.ds(0, 8)], wc_ref.at[1 - dc, :, pl.ds(CL + 8, 8)]),
            ]
        for i, (src, dst) in enumerate(pieces):
            halo.append(remote(src, dst, hs_sem.at[k, i], hr_sem.at[k, i], target))
    for c in halo:
        c.start()

    loads[1].wait()
    loads[2].wait()
    lane_of = lax.shift_right_logical(lax.broadcasted_iota(jnp.int32, (R, 4 * K), 1), 5)
    for j in range(CL // 4):
        left = wr_ref[1, 1 + 4 * j : 5 + 4 * j].reshape(4 * R, PS)
        right = bas[4 * j : 4 * j + 4].reshape(4 * K, PS)
        full = lax.dot_general(left, right, (((1,), (1,)), ((), ())), preferred_element_type=F32)
        mine = jnp.zeros((R, 4 * K), F32)
        for i in range(4):
            mine = mine + jnp.where(lane_of == i, full[i * R : (i + 1) * R, :], 0.0)
        every[row, cy, core, j] = mine.astype(BF)

    first = []
    for k in (1, 2, 3):
        ref = every.at[row, cy, core]
        first.append(remote(ref, ref, g1s.at[k - 1], g1r.at[k - 1], place(row, col + 2 * k)))
    for c in first:
        c.start()

    loads[0].wait()
    steps = lax.broadcasted_iota(jnp.int32, (CL, PS), 0) + row * CL
    ox = own_c[0] - (steps.astype(F32) + 0.5)
    oy = own_c[1] - (col.astype(F32) + 0.5)
    oz = own_c[2]
    on = GAIN * (ox * ox + oy * oy + oz * oz)
    for i, v in enumerate((ox, oy, oz, on)):
        v = v.T
        for g in range(CL):
            tables[g, i] = jnp.broadcast_to(v[:, g : g + 1], (PS, 128))

    for c in first:
        c.wait()
    second = []
    for k in range(1, NR):
        ref = every.at[row, :, core]
        second.append(remote(ref, ref, g2s.at[k - 1], g2r.at[k - 1], place(row + k, col)))
    for c in second:
        c.start()

    loads[4].wait()
    for c in halo:
        c.wait()

    tiles = (tile0, tile1)
    build = functools.partial(
        make_tile, pairs=pairs, tables=tables, wc_ref=wc_ref, row0=row, col0=col
    )
    use = functools.partial(use_tile, pairs=pairs, wr_ref=wr_ref, f_ref=f_ref, b_ref=b_ref)

    def sweep(lo, hi):
        @pl.loop(lo, hi)
        def _(i):
            for j in range(2):

                @pl.when(i < NP + j)
                def _():
                    s = 2 * i + j
                    use(s, tiles[j])
                    build(jnp.minimum(s + 1, NP - 1), tiles[1 - j])

    build(0, tile0)
    cut = NP // 2 * 3 // 4
    sweep(0, cut)
    for c in second:
        c.wait()
    ref = every.at[:, :, core]
    third = remote(ref, ref, g3s.at[0], g3r.at[0], (row, col + 1 - 2 * core))
    third.start()
    sweep(cut, NP // 2)

    fwd, bwd = slot_codes(pairs_v)
    terms = b_ref[...]
    back = []

    def give(k):
        dr, dc = NEIGHBOURS[k]
        target = place(row + dr, col + dc)
        if dr == 0:
            src, dst = send.at[dc + 1, pl.ds(1, CL)], back_c.at[k]
        else:
            src = send.at[dc + 1, pl.ds(0 if dr < 0 else CL + 1, 1)]
            dst = back_r.at[pl.ds(k - 2, 1)]
        c = remote(src, dst, bs_sem.at[k], br_sem.at[k], target)
        c.start()
        back.append(c)

    wide = (CL + 2) * R
    for dc, ks in ((-1, (0, 2, 5)), (1, (1, 4, 7))):
        part = jnp.dot(one_hot(bwd, (dc + 1) * wide, wide), terms, preferred_element_type=F32)
        send[dc + 1] = part.astype(BF).reshape(CL + 2, R, PS)
        for k in ks:
            give(k)
    for at, k in ((0, 3), (CL + 1, 6)):
        part = jnp.dot(one_hot(bwd, wide + at * R, R), terms, preferred_element_type=F32)
        send[1, at] = part.astype(BF)
        give(k)
    near = jnp.dot(one_hot(bwd, wide + R, CL * R), terms, preferred_element_type=F32)
    near = near + jnp.dot(one_hot(fwd, 0, CL * R), f_ref[...], preferred_element_type=F32)
    out[...] = near.reshape(CL, R, PS)

    third.wait()
    loads[3].wait()

    @pl.loop(0, CL)
    def _(g):
        blocks = []
        for f in range(0, FAR, 4):
            mine = jnp.zeros((R, 4 * K), F32)
            for j in range(4):
                h = far[g, f + j]
                d = h // CL
                got = every[d // NC, (d % NC) // 2, d % 2, (h % CL) // 4].astype(F32)
                got = pltpu.roll(got, ((j - h % 4 + 4) % 4) * K, 1)
                mine = jnp.where(lane_of == j, got, mine)
            blocks.append(mine.astype(BF))
        z = jnp.dot(jnp.concatenate(blocks, axis=1), cpl[g], preferred_element_type=F32)
        out[g] += jnp.dot(z.astype(BF), bas[g], preferred_element_type=F32)

    for c in back:
        c.wait()
    out[...] += back_c[0].astype(F32) + back_c[1].astype(F32)
    out[CL - 1] += back_r[0].astype(F32) + back_r[1].astype(F32) + back_r[2].astype(F32)
    out[0] += back_r[3].astype(F32) + back_r[4].astype(F32) + back_r[5].astype(F32)


def per_device(coords, rhs, near_pairs, far_list, basis, coupling):
    smem = pl.BlockSpec(memory_space=pltpu.SMEM)
    vmem = pl.BlockSpec(memory_space=pltpu.VMEM)
    hbm = pl.BlockSpec(memory_space=pl.ANY)
    dma = pltpu.SemaphoreType.DMA
    pairs = near_pairs.T
    return pl.pallas_call(
        body,
        out_shape=jax.ShapeDtypeStruct((CL, R, PS), F32),
        in_specs=[smem, smem, vmem, hbm, hbm, hbm, hbm],
        out_specs=vmem,
        scratch_shapes=[
            pltpu.VMEM((3, CL, PS), F32),
            pltpu.VMEM((3, 3, CL + 16, PS), F32),
            pltpu.VMEM((3, CL + 2, R, PS), BF),
            pltpu.VMEM((CL, K, PS), BF),
            pltpu.VMEM((CL, FAR * K, K), BF),
            pltpu.VMEM((CL, 4, PS, 128), F32),
            pltpu.VMEM((NR, NC // 2, 2, CL // 4, R, 4 * K), BF),
            pltpu.VMEM((PS, PS), BF),
            pltpu.VMEM((PS, PS), BF),
            pltpu.VMEM((NP * R, PS), BF),
            pltpu.VMEM((NP * R, PS), BF),
            pltpu.VMEM((3, CL + 2, R, PS), BF),
            pltpu.VMEM((2, CL, R, PS), BF),
            pltpu.VMEM((6, R, PS), BF),
            dma((5,)),
            dma((8, 2)),
            dma((8, 2)),
            dma((3,)),
            dma((3,)),
            dma((NR - 1,)),
            dma((NR - 1,)),
            dma((1,)),
            dma((1,)),
            dma((8,)),
            dma((8,)),
        ],
        compiler_params=pltpu.CompilerParams(
            collective_id=0, has_side_effects=True, vmem_limit_bytes=52 * 2**20
        ),
        name="hmatrix",
    )(
        pairs,
        far_list,
        pairs,
        coords.transpose(1, 0, 2),
        rhs,
        basis,
        coupling.reshape(CL, FAR * K, K),
    )


def solution(mesh):
    return jax.shard_map(
        per_device,
        mesh=mesh,
        in_specs=(
            P(("row", "col"), None, None),
            P(("row", "col"), None, None),
            P(("row", "col"), None),
            P(("row", "col"), None),
            P(("row", "col"), None, None),
            P(("row", "col"), None, None, None),
        ),
        out_specs=P(("row", "col"), None, None),
        check_vma=False,
    )
```

```python
import functools

import jax
import jax.numpy as jnp
from jax import lax
from jax.experimental import pallas as pl
from jax.experimental.pallas import tpu as pltpu
from jax.sharding import PartitionSpec as P

MESH = pl.DeviceIdType.MESH
BF = jnp.bfloat16
F32 = jnp.float32
SOFTEN = 0.0025
GAIN = 256.0

NR, NC = 16, 8
CL, R, PS, K, FAR, NP = 16, 16, 512, 32, 32, 64
CHUNK = 64
NEIGHBOURS = [(0, -1), (0, 1), (-1, -1), (-1, 0), (-1, 1), (1, -1), (1, 0), (1, 1)]


def place(row, col):
    return (lax.rem(row + NR, NR), lax.rem(col + NC, NC))


def pair_ids(pairs, s):
    a = pairs[0, s]
    b = pairs[1, s]
    b = jnp.where(b < 0, 4 * CL + a, b)
    o = lax.shift_right_logical(b, 4)
    l = lax.bitwise_and(b, CL - 1)
    down = lax.shift_right_logical(o * 11, 5)
    wr = jnp.clip(1 - CL + down * CL + l, 0, CL + 1)
    return a, o - 3 * down, wr


def make_tile(s, tile, pairs, tables, wc_ref, row0, col0):
    a, wc, wr = pair_ids(pairs, s)
    x0 = (row0 * CL + a).astype(F32) + 0.5
    y0 = col0.astype(F32) + 0.5
    at = pl.ds(wr + 7, 1)
    bx = wc_ref[wc, 0, at, :] - x0
    by = wc_ref[wc, 1, at, :] - y0
    bz = wc_ref[wc, 2, at, :]
    nb = GAIN * (bx * bx + by * by + bz * bz + SOFTEN)
    bx, by, bz = (-2.0 * GAIN) * bx, (-2.0 * GAIN) * by, (-2.0 * GAIN) * bz
    bx, by, bz, nb = [jnp.broadcast_to(v, (8, PS)) for v in (bx, by, bz, nb)]
    for p in range(0, PS, 16):
        for q in range(0, PS, 128):
            ql = slice(q, q + 128)
            halves = []
            for h in (p, p + 8):
                ax, ay, az, na = [tables[a, i, h : h + 8, :] for i in range(4)]
                sq = (na + nb[:, ql]) + ax * bx[:, ql]
                sq = sq + (ay * by[:, ql] + az * bz[:, ql])
                halves.append(lax.rsqrt(sq))
            tile[p : p + 16, ql] = jnp.concatenate(halves, axis=0).astype(BF)


def use_tile(s, tile, pairs, wr_ref, f_ref, b_ref):
    a, wc, wr = pair_ids(pairs, s)
    left = wr_ref[1, a + 1]
    right = wr_ref[wc, wr]
    t = tile[...]
    rows = pl.ds(pl.multiple_of(s * R, R), R)
    f_ref[rows, :] = lax.dot_general(
        right, t, (((1,), (1,)), ((), ())), preferred_element_type=F32
    ).astype(BF)
    b_ref[rows, :] = jnp.dot(left, t, preferred_element_type=F32).astype(BF)


def one_hot(codes, first, count):
    rows = lax.broadcasted_iota(jnp.int32, (count, NP * R), 0) + first
    return jnp.where(rows == codes, 1.0, 0.0).astype(BF)


def slot_codes(pairs_v):
    a = pairs_v[0:1, :]
    b = pairs_v[1:2, :]
    alive = b >= 0
    b = jnp.maximum(b, 0)
    o = lax.shift_right_logical(b, 4)
    l = lax.bitwise_and(b, 15)
    down = jnp.where(o >= 6, 2, jnp.where(o >= 3, 1, 0))
    wc = o - 3 * down
    wr = (down - 1) * CL + l + 1
    same = jnp.logical_and(o == 4, l == a)
    fwd = jnp.where(alive, a, -1)
    bwd = jnp.where(jnp.logical_and(alive, jnp.logical_not(same)), wc * (CL + 2) + wr, -1)
    slot = lax.broadcasted_iota(jnp.int32, (NP, NP * R), 0)
    lane = lax.broadcasted_iota(jnp.int32, (NP, NP * R), 1)
    spread = jnp.where(lax.shift_right_logical(lane, 4) == slot, 1.0, 0.0).astype(BF)
    inner = lax.bitwise_and(lax.broadcasted_iota(jnp.int32, (1, NP * R), 1), 15)
    out = []
    for v in (fwd, bwd):
        v = jnp.broadcast_to(v, (8, NP)).astype(F32).astype(BF)
        v = jnp.dot(v, spread, preferred_element_type=F32)[0:1, :]
        out.append(v.astype(jnp.int32) * R + inner)
    return out


def body(
    pairs, far, pairs_v, coords, rhs, basis, coupling, out,
    own_c, wc_ref, wr_ref, bas, cpl, tables, every, tile0, tile1, f_ref, b_ref,
    send, back_c, back_r,
    loc_sem, hs_sem, hr_sem, g1s, g1r, g2s, g2r, g3s, g3r, bs_sem, br_sem,
):
    row = lax.axis_index("row")
    col = lax.axis_index("col")
    core = lax.rem(col, 2)
    cy = col // 2

    loads = [
        pltpu.make_async_copy(coords, own_c, loc_sem.at[0]),
        pltpu.make_async_copy(rhs, wr_ref.at[1, pl.ds(1, CL)], loc_sem.at[1]),
        pltpu.make_async_copy(basis, bas, loc_sem.at[2]),
        pltpu.make_async_copy(coupling, cpl, loc_sem.at[3]),
        pltpu.make_async_copy(coords, wc_ref.at[1, :, pl.ds(8, CL)], loc_sem.at[4]),
    ]
    for i in (0, 1, 2, 4):
        loads[i].start()

    barrier = pltpu.get_barrier_semaphore()
    partners = [place(row + dr, col + dc) for dr, dc in NEIGHBOURS if dc]
    partners += [place(row, col + 2 * k) for k in (1, 2, 3)]
    partners += [place(row + k, col) for k in range(1, NR)]
    for target in partners:
        pl.semaphore_signal(barrier, inc=1, device_id=target, device_id_type=MESH)

    pl.semaphore_wait(barrier, len(partners))

    def remote(src, dst, s, r, target):
        return pltpu.make_async_remote_copy(
            src_ref=src, dst_ref=dst, send_sem=s, recv_sem=r, device_id=target, device_id_type=MESH
        )

    halo = []
    for k, (dr, dc) in enumerate(NEIGHBOURS):
        target = place(row + dr, col + dc)
        if dr == 0:
            pieces = [
                (rhs, wr_ref.at[1 - dc, pl.ds(1, CL)]),
                (coords, wc_ref.at[1 - dc, :, pl.ds(8, CL)]),
            ]
        elif dr == 1:
            pieces = [
                (rhs.at[pl.ds(CL - 1, 1)], wr_ref.at[1 - dc, pl.ds(0, 1)]),
                (coords.at[:, pl.ds(CL - 8, 8)], wc_ref.at[1 - dc, :, pl.ds(0, 8)]),
            ]
        else:
            pieces = [
                (rhs.at[pl.ds(0, 1)], wr_ref.at[1 - dc, pl.ds(CL + 1, 1)]),
                (coords.at[:, pl.ds(0, 8)], wc_ref.at[1 - dc, :, pl.ds(CL + 8, 8)]),
            ]
        for i, (src, dst) in enumerate(pieces):
            halo.append(remote(src, dst, hs_sem.at[k, i], hr_sem.at[k, i], target))
    for c in halo:
        c.start()
    loads[3].start()

    loads[1].wait()
    loads[2].wait()
    lane_of = lax.shift_right_logical(lax.broadcasted_iota(jnp.int32, (R, 4 * K), 1), 5)
    for j in range(CL // 4):
        left = wr_ref[1, 1 + 4 * j : 5 + 4 * j].reshape(4 * R, PS)
        right = bas[4 * j : 4 * j + 4].reshape(4 * K, PS)
        full = lax.dot_general(left, right, (((1,), (1,)), ((), ())), preferred_element_type=F32)
        mine = jnp.zeros((R, 4 * K), F32)
        for i in range(4):
            mine = mine + jnp.where(lane_of == i, full[i * R : (i + 1) * R, :], 0.0)
        every[row * (NC // 2) + cy, core * 4 + j] = mine.astype(BF)

    first = []
    for k in (1, 2, 3):
        ref = every.at[row * (NC // 2) + cy, pl.ds(core * 4, 4)]
        first.append(remote(ref, ref, g1s.at[k - 1], g1r.at[k - 1], place(row, col + 2 * k)))
    for c in first:
        c.start()

    loads[0].wait()
    steps = lax.broadcasted_iota(jnp.int32, (CL, PS), 0) + row * CL
    ox = own_c[0] - (steps.astype(F32) + 0.5)
    oy = own_c[1] - (col.astype(F32) + 0.5)
    oz = own_c[2]
    on = GAIN * (ox * ox + oy * oy + oz * oz)
    for i, v in enumerate((ox, oy, oz, on)):
        v = v.T
        for g in range(CL):
            tables[g, i] = jnp.broadcast_to(v[:, g : g + 1], (PS, 128))

    loads[4].wait()
    for c in halo:
        c.wait()
    tiles = (tile0, tile1)
    build = functools.partial(
        make_tile, pairs=pairs, tables=tables, wc_ref=wc_ref, row0=row, col0=col
    )
    use = functools.partial(use_tile, pairs=pairs, wr_ref=wr_ref, f_ref=f_ref, b_ref=b_ref)

    def sweep(lo, hi):
        @pl.loop(lo, hi)
        def _(i):
            for j in range(2):

                @pl.when(i < NP + j)
                def _():
                    s = 2 * i + j
                    use(s, tiles[j])
                    build(jnp.minimum(s + 1, NP - 1), tiles[1 - j])

    build(0, tile0)
    sweep(0, 3)
    for c in first:
        c.wait()
    second = []
    for k in range(1, NR):
        ref = every.at[pl.ds(row * (NC // 2), NC // 2), pl.ds(core * 4, 4)]
        second.append(remote(ref, ref, g2s.at[k - 1], g2r.at[k - 1], place(row + k, col)))
    for c in second:
        c.start()
    sweep(3, 28)
    for c in second:
        c.wait()
    ref = every.at[:, pl.ds(core * 4, 4)]
    third = remote(ref, ref, g3s.at[0], g3r.at[0], (row, col + 1 - 2 * core))
    third.start()
    sweep(28, NP // 2)

    fwd, bwd = slot_codes(pairs_v)
    terms = b_ref[...]
    back = []

    def give(k):
        dr, dc = NEIGHBOURS[k]
        target = place(row + dr, col + dc)
        if dr == 0:
            src, dst = send.at[dc + 1, pl.ds(1, CL)], back_c.at[k]
        else:
            src = send.at[dc + 1, pl.ds(0 if dr < 0 else CL + 1, 1)]
            dst = back_r.at[pl.ds(k - 2, 1)]
        c = remote(src, dst, bs_sem.at[k], br_sem.at[k], target)
        c.start()
        back.append(c)

    wide = (CL + 2) * R
    for dc, ks in ((-1, (0, 2, 5)), (1, (1, 4, 7))):
        part = jnp.dot(one_hot(bwd, (dc + 1) * wide, wide), terms, preferred_element_type=F32)
        send[dc + 1] = part.astype(BF).reshape(CL + 2, R, PS)
        for k in ks:
            give(k)
    for at, k in ((0, 3), (CL + 1, 6)):
        part = jnp.dot(one_hot(bwd, wide + at * R, R), terms, preferred_element_type=F32)
        send[1, at] = part.astype(BF)
        give(k)
    near = jnp.dot(one_hot(bwd, wide + R, CL * R), terms, preferred_element_type=F32)
    near = near + jnp.dot(one_hot(fwd, 0, CL * R), f_ref[...], preferred_element_type=F32)
    out[...] = near.reshape(CL, R, PS)

    third.wait()
    loads[3].wait()

    @pl.loop(0, CL, unroll=2)
    def _(g):
        blocks = []
        for f in range(0, FAR, 4):
            mine = jnp.zeros((R, 4 * K), F32)
            for j in range(4):
                h = far[g, f + j]
                at = lax.bitwise_and(lax.shift_right_logical(h, 2), 7)
                got = every[lax.shift_right_logical(h, 5), at].astype(F32)
                got = pltpu.roll(got, lax.bitwise_and(j - h, 3) * K, 1)
                mine = jnp.where(lane_of == j, got, mine)
            blocks.append(mine.astype(BF))
        z = jnp.dot(jnp.concatenate(blocks, axis=1), cpl[g], preferred_element_type=F32)
        out[g] += jnp.dot(z.astype(BF), bas[g], preferred_element_type=F32)

    for c in back:
        c.wait()
    out[...] += back_c[0].astype(F32) + back_c[1].astype(F32)
    out[CL - 1] += back_r[0].astype(F32) + back_r[1].astype(F32) + back_r[2].astype(F32)
    out[0] += back_r[3].astype(F32) + back_r[4].astype(F32) + back_r[5].astype(F32)


def per_device(coords, rhs, near_pairs, far_list, basis, coupling):
    smem = pl.BlockSpec(memory_space=pltpu.SMEM)
    vmem = pl.BlockSpec(memory_space=pltpu.VMEM)
    hbm = pl.BlockSpec(memory_space=pltpu.HBM)
    dma = pltpu.SemaphoreType.DMA
    pairs = near_pairs.T
    return pl.pallas_call(
        body,
        out_shape=jax.ShapeDtypeStruct((CL, R, PS), F32),
        in_specs=[smem, smem, vmem, hbm, hbm, hbm, hbm],
        out_specs=vmem,
        scratch_shapes=[
            pltpu.VMEM((3, CL, PS), F32),
            pltpu.VMEM((3, 3, CL + 16, PS), F32),
            pltpu.VMEM((3, CL + 2, R, PS), BF),
            pltpu.VMEM((CL, K, PS), BF),
            pltpu.VMEM((CL, FAR * K, K), BF),
            pltpu.VMEM((CL, 4, PS, 128), F32),
            pltpu.VMEM((NR * NC // 2, 2 * CL // 4, R, 4 * K), BF),
            pltpu.VMEM((PS, PS), BF),
            pltpu.VMEM((PS, PS), BF),
            pltpu.VMEM((NP * R, PS), BF),
            pltpu.VMEM((NP * R, PS), BF),
            pltpu.VMEM((3, CL + 2, R, PS), BF),
            pltpu.VMEM((2, CL, R, PS), BF),
            pltpu.VMEM((6, R, PS), BF),
            dma((5,)),
            dma((8, 2)),
            dma((8, 2)),
            dma((3,)),
            dma((3,)),
            dma((NR - 1,)),
            dma((NR - 1,)),
            dma((1,)),
            dma((1,)),
            dma((8,)),
            dma((8,)),
        ],
        compiler_params=pltpu.CompilerParams(
            collective_id=0, has_side_effects=True, vmem_limit_bytes=63 * 2**20
        ),
        name="hmatrix",
    )(
        pairs,
        far_list,
        pairs,
        coords.transpose(1, 0, 2),
        rhs,
        basis,
        coupling.reshape(CL, FAR * K, K),
    )


def solution(mesh):
    return jax.shard_map(
        per_device,
        mesh=mesh,
        in_specs=(
            P(("row", "col"), None, None),
            P(("row", "col"), None, None),
            P(("row", "col"), None),
            P(("row", "col"), None),
            P(("row", "col"), None, None),
            P(("row", "col"), None, None, None),
        ),
        out_specs=P(("row", "col"), None, None),
        check_vma=False,
    )
```

```python
import functools

import jax
import jax.numpy as jnp
from jax import lax
from jax.experimental import pallas as pl
from jax.experimental.pallas import tpu as pltpu
from jax.sharding import PartitionSpec as P

MESH = pl.DeviceIdType.MESH
BF = jnp.bfloat16
F32 = jnp.float32
SOFTEN = 0.0025
GAIN = 256.0

NR, NC = 16, 8
CL, R, PS, K, FAR, NP = 16, 16, 512, 32, 32, 64
CHUNK = 64
NEIGHBOURS = [(0, -1), (0, 1), (-1, -1), (-1, 0), (-1, 1), (1, -1), (1, 0), (1, 1)]


def place(row, col):
    return (lax.rem(row + NR, NR), lax.rem(col + NC, NC))


def pair_ids(pairs, s):
    a = pairs[0, s]
    b = pairs[1, s]
    b = jnp.where(b < 0, 4 * CL + a, b)
    o = lax.shift_right_logical(b, 4)
    l = lax.bitwise_and(b, CL - 1)
    down = lax.shift_right_logical(o * 11, 5)
    wr = jnp.clip(1 - CL + down * CL + l, 0, CL + 1)
    return a, o - 3 * down, wr


def make_tile(s, tile, pairs, tables, wc_ref, row0, col0):
    a, wc, wr = pair_ids(pairs, s)
    x0 = (row0 * CL + a).astype(F32) + 0.5
    y0 = col0.astype(F32) + 0.5
    at = pl.ds(wr + 7, 1)
    bx = wc_ref[wc, 0, at, :] - x0
    by = wc_ref[wc, 1, at, :] - y0
    bz = wc_ref[wc, 2, at, :]
    nb = GAIN * (bx * bx + by * by + bz * bz + SOFTEN)
    bx, by, bz = (-2.0 * GAIN) * bx, (-2.0 * GAIN) * by, (-2.0 * GAIN) * bz
    bx, by, bz, nb = [jnp.broadcast_to(v, (8, PS)) for v in (bx, by, bz, nb)]
    for p in range(0, PS, 16):
        for q in range(0, PS, 128):
            ql = slice(q, q + 128)
            halves = []
            for h in (p, p + 8):
                ax, ay, az, na = [tables[a, i, h : h + 8, :] for i in range(4)]
                sq = (na + nb[:, ql]) + ax * bx[:, ql]
                sq = sq + (ay * by[:, ql] + az * bz[:, ql])
                halves.append(lax.rsqrt(sq))
            tile[p : p + 16, ql] = jnp.concatenate(halves, axis=0).astype(BF)


def use_tile(s, tile, pairs, wr_ref, f_ref, b_ref):
    a, wc, wr = pair_ids(pairs, s)
    left = wr_ref[1, a + 1]
    right = wr_ref[wc, wr]
    t = tile[...]
    rows = pl.ds(pl.multiple_of(s * R, R), R)
    f_ref[rows, :] = lax.dot_general(
        right, t, (((1,), (1,)), ((), ())), preferred_element_type=F32
    ).astype(BF)
    b_ref[rows, :] = jnp.dot(left, t, preferred_element_type=F32).astype(BF)


def one_hot(codes, first, count):
    rows = lax.broadcasted_iota(jnp.int32, (count, NP * R), 0) + first
    return jnp.where(rows == codes, 1.0, 0.0).astype(BF)


def slot_codes(pairs_v):
    a = pairs_v[0:1, :]
    b = pairs_v[1:2, :]
    alive = b >= 0
    b = jnp.maximum(b, 0)
    o = lax.shift_right_logical(b, 4)
    l = lax.bitwise_and(b, 15)
    down = jnp.where(o >= 6, 2, jnp.where(o >= 3, 1, 0))
    wc = o - 3 * down
    wr = (down - 1) * CL + l + 1
    same = jnp.logical_and(o == 4, l == a)
    fwd = jnp.where(alive, a, -1)
    bwd = jnp.where(jnp.logical_and(alive, jnp.logical_not(same)), wc * (CL + 2) + wr, -1)
    slot = lax.broadcasted_iota(jnp.int32, (NP, NP * R), 0)
    lane = lax.broadcasted_iota(jnp.int32, (NP, NP * R), 1)
    spread = jnp.where(lax.shift_right_logical(lane, 4) == slot, 1.0, 0.0).astype(BF)
    inner = lax.bitwise_and(lax.broadcasted_iota(jnp.int32, (1, NP * R), 1), 15)
    out = []
    for v in (fwd, bwd):
        v = jnp.broadcast_to(v, (8, NP)).astype(F32).astype(BF)
        v = jnp.dot(v, spread, preferred_element_type=F32)[0:1, :]
        out.append(v.astype(jnp.int32) * R + inner)
    return out


def body(
    pairs_h, far_h, coords, rhs, basis, coupling, out,
    pairs, far, pairs_v, own_c, wc_ref, wr_ref, bas, cpl, tables, every, tile0, tile1, f_ref, b_ref,
    send, back_c, back_r,
    loc_sem, hs_sem, hr_sem, g1s, g1r, g2s, g2r, g3s, g3r, bs_sem, br_sem,
):
    row = lax.axis_index("row")
    col = lax.axis_index("col")
    core = lax.rem(col, 2)
    cy = col // 2

    loads = [
        pltpu.make_async_copy(coords, own_c, loc_sem.at[0]),
        pltpu.make_async_copy(rhs, wr_ref.at[1, pl.ds(1, CL)], loc_sem.at[1]),
        pltpu.make_async_copy(basis, bas, loc_sem.at[2]),
        pltpu.make_async_copy(coupling, cpl, loc_sem.at[3]),
        pltpu.make_async_copy(coords, wc_ref.at[1, :, pl.ds(8, CL)], loc_sem.at[4]),
        pltpu.make_async_copy(pairs_h, pairs, loc_sem.at[5]),
        pltpu.make_async_copy(far_h, far, loc_sem.at[6]),
        pltpu.make_async_copy(pairs_h, pairs_v, loc_sem.at[7]),
    ]

    barrier = pltpu.get_barrier_semaphore()
    partners = [place(row + dr, col + dc) for dr, dc in NEIGHBOURS if dc]
    partners += [place(row, col + 2 * k) for k in (1, 2, 3)]
    partners += [place(row + k, col) for k in range(1, NR)]
    for target in partners:
        pl.semaphore_signal(barrier, inc=1, device_id=target, device_id_type=MESH)
    for i in (0, 1, 2, 4, 5, 6, 7):
        loads[i].start()

    pl.semaphore_wait(barrier, len(partners))

    def remote(src, dst, s, r, target):
        return pltpu.make_async_remote_copy(
            src_ref=src, dst_ref=dst, send_sem=s, recv_sem=r, device_id=target, device_id_type=MESH
        )

    halo = []
    for k, (dr, dc) in enumerate(NEIGHBOURS):
        target = place(row + dr, col + dc)
        if dr == 0:
            pieces = [
                (rhs, wr_ref.at[1 - dc, pl.ds(1, CL)]),
                (coords, wc_ref.at[1 - dc, :, pl.ds(8, CL)]),
            ]
        elif dr == 1:
            pieces = [
                (rhs.at[pl.ds(CL - 1, 1)], wr_ref.at[1 - dc, pl.ds(0, 1)]),
                (coords.at[:, pl.ds(CL - 1, 1)], wc_ref.at[1 - dc, :, pl.ds(7, 1)]),
            ]
        else:
            pieces = [
                (rhs.at[pl.ds(0, 1)], wr_ref.at[1 - dc, pl.ds(CL + 1, 1)]),
                (coords.at[:, pl.ds(0, 1)], wc_ref.at[1 - dc, :, pl.ds(CL + 8, 1)]),
            ]
        for i, (src, dst) in enumerate(pieces):
            halo.append(remote(src, dst, hs_sem.at[k, i], hr_sem.at[k, i], target))
    for c in halo:
        c.start()
    loads[3].start()

    loads[1].wait()
    loads[2].wait()
    lane_of = lax.shift_right_logical(lax.broadcasted_iota(jnp.int32, (R, 4 * K), 1), 5)
    for j in range(CL // 4):
        left = wr_ref[1, 1 + 4 * j : 5 + 4 * j].reshape(4 * R, PS)
        right = bas[4 * j : 4 * j + 4].reshape(4 * K, PS)
        full = lax.dot_general(left, right, (((1,), (1,)), ((), ())), preferred_element_type=F32)
        mine = jnp.zeros((R, 4 * K), F32)
        for i in range(4):
            mine = mine + jnp.where(lane_of == i, full[i * R : (i + 1) * R, :], 0.0)
        every[row * (NC // 2) + cy, core * 4 + j] = mine.astype(BF)

    first = []
    for k in (1, 2, 3):
        ref = every.at[row * (NC // 2) + cy, pl.ds(core * 4, 4)]
        first.append(remote(ref, ref, g1s.at[k - 1], g1r.at[k - 1], place(row, col + 2 * k)))
    for c in first:
        c.start()

    loads[0].wait()
    steps = lax.broadcasted_iota(jnp.int32, (CL, PS), 0) + row * CL
    ox = own_c[0] - (steps.astype(F32) + 0.5)
    oy = own_c[1] - (col.astype(F32) + 0.5)
    oz = own_c[2]
    on = GAIN * (ox * ox + oy * oy + oz * oz)
    for i, v in enumerate((ox, oy, oz, on)):
        v = v.T
        for g in range(CL):
            tables[g, i] = jnp.broadcast_to(v[:, g : g + 1], (PS, 128))

    loads[4].wait()
    loads[5].wait()
    for c in halo:
        c.wait()
    tiles = (tile0, tile1)
    build = functools.partial(
        make_tile, pairs=pairs, tables=tables, wc_ref=wc_ref, row0=row, col0=col
    )
    use = functools.partial(use_tile, pairs=pairs, wr_ref=wr_ref, f_ref=f_ref, b_ref=b_ref)

    def sweep(lo, hi):
        @pl.loop(lo, hi)
        def _(i):
            for j in range(2):

                @pl.when(i < NP + j)
                def _():
                    s = 2 * i + j
                    use(s, tiles[j])
                    build(s + 1, tiles[1 - j])

    build(0, tile0)
    sweep(0, 3)
    for c in first:
        c.wait()
    second = []
    for k in range(1, NR):
        ref = every.at[pl.ds(row * (NC // 2), NC // 2), pl.ds(core * 4, 4)]
        second.append(remote(ref, ref, g2s.at[k - 1], g2r.at[k - 1], place(row + k, col)))
    for c in second:
        c.start()
    sweep(3, 28)
    for c in second:
        c.wait()
    ref = every.at[:, pl.ds(core * 4, 4)]
    third = remote(ref, ref, g3s.at[0], g3r.at[0], (row, col + 1 - 2 * core))
    third.start()
    sweep(28, NP // 2 - 1)
    use(NP - 2, tile0)
    build(NP - 1, tile1)
    use(NP - 1, tile1)

    loads[7].wait()
    fwd, bwd = slot_codes(pairs_v[...])
    terms = b_ref[...]
    back = []

    def give(k, dr, dc):
        if dr == 0:
            src, dst = send.at[dc + 1, pl.ds(1, CL)], back_c.at[k]
        else:
            src = send.at[dc + 1, pl.ds(0 if dr < 0 else CL + 1, 1)]
            dst = back_r.at[pl.ds(k - 2, 1)]
        c = remote(src, dst, bs_sem.at[k], br_sem.at[k], place(row + dr, col + dc))
        c.start()
        back.append(c)

    wide = (CL + 2) * R
    for side in (core, 1 - core):
        dc = 2 * side - 1
        part = jnp.dot(one_hot(bwd, (dc + 1) * wide, wide), terms, preferred_element_type=F32)
        send[dc + 1] = part.astype(BF).reshape(CL + 2, R, PS)
        give(side, 0, dc)
        give(2 + 2 * side, -1, dc)
        give(5 + 2 * side, 1, dc)
    for at, k, dr in ((0, 3, -1), (CL + 1, 6, 1)):
        part = jnp.dot(one_hot(bwd, wide + at * R, R), terms, preferred_element_type=F32)
        send[1, at] = part.astype(BF)
        give(k, dr, 0)
    near = jnp.dot(one_hot(bwd, wide + R, CL * R), terms, preferred_element_type=F32)
    near = near + jnp.dot(one_hot(fwd, 0, CL * R), f_ref[...], preferred_element_type=F32)
    out[...] = near.reshape(CL, R, PS)

    third.wait()
    loads[3].wait()
    loads[6].wait()

    @pl.loop(0, CL, unroll=4)
    def _(g):
        blocks = []
        for f in range(0, FAR, 4):
            mine = jnp.zeros((R, 4 * K), F32)
            for j in range(4):
                h = far[g, f + j]
                at = lax.bitwise_and(lax.shift_right_logical(h, 2), 7)
                got = every[lax.shift_right_logical(h, 5), at].astype(F32)
                got = pltpu.roll(got, lax.bitwise_and(j - h, 3) * K, 1)
                mine = jnp.where(lane_of == j, got, mine)
            blocks.append(mine.astype(BF))
        z = jnp.dot(jnp.concatenate(blocks, axis=1), cpl[g], preferred_element_type=F32)
        out[g] += jnp.dot(z.astype(BF), bas[g], preferred_element_type=F32)

    for c in back:
        c.wait()
    out[...] += back_c[0].astype(F32) + back_c[1].astype(F32)
    out[CL - 1] += back_r[0].astype(F32) + back_r[1].astype(F32) + back_r[2].astype(F32)
    out[0] += back_r[3].astype(F32) + back_r[4].astype(F32) + back_r[5].astype(F32)


def per_device(coords, rhs, near_pairs, far_list, basis, coupling):
    vmem = pl.BlockSpec(memory_space=pltpu.VMEM)
    hbm = pl.BlockSpec(memory_space=pltpu.HBM)
    dma = pltpu.SemaphoreType.DMA
    def hold(x):
        return pltpu.with_memory_space_constraint(x, pltpu.HBM)

    return pl.pallas_call(
        body,
        out_shape=pltpu.VMEM((CL, R, PS), F32),
        in_specs=[hbm] * 6,
        out_specs=vmem,
        scratch_shapes=[
            pltpu.SMEM((2, NP), jnp.int32),
            pltpu.SMEM((CL, FAR), jnp.int32),
            pltpu.VMEM((2, NP), jnp.int32),
            pltpu.VMEM((3, CL, PS), F32),
            pltpu.VMEM((3, 3, CL + 16, PS), F32),
            pltpu.VMEM((3, CL + 2, R, PS), BF),
            pltpu.VMEM((CL, K, PS), BF),
            pltpu.VMEM((CL, FAR * K, K), BF),
            pltpu.VMEM((CL, 4, PS, 128), F32),
            pltpu.VMEM((NR * NC // 2, 2 * CL // 4, R, 4 * K), BF),
            pltpu.VMEM((PS, PS), BF),
            pltpu.VMEM((PS, PS), BF),
            pltpu.VMEM((NP * R, PS), BF),
            pltpu.VMEM((NP * R, PS), BF),
            pltpu.VMEM((3, CL + 2, R, PS), BF),
            pltpu.VMEM((2, CL, R, PS), BF),
            pltpu.VMEM((6, R, PS), BF),
            dma((8,)),
            dma((8, 2)),
            dma((8, 2)),
            dma((3,)),
            dma((3,)),
            dma((NR - 1,)),
            dma((NR - 1,)),
            dma((1,)),
            dma((1,)),
            dma((8,)),
            dma((8,)),
        ],
        compiler_params=pltpu.CompilerParams(
            collective_id=0, has_side_effects=True, vmem_limit_bytes=62 * 2**20
        ),
        name="hmatrix",
    )(
        hold(near_pairs.T),
        hold(far_list),
        hold(coords.transpose(1, 0, 2)),
        hold(rhs),
        hold(basis),
        hold(coupling.reshape(CL, FAR * K, K)),
    )


def solution(mesh):
    return jax.shard_map(
        per_device,
        mesh=mesh,
        in_specs=(
            P(("row", "col"), None, None),
            P(("row", "col"), None, None),
            P(("row", "col"), None),
            P(("row", "col"), None),
            P(("row", "col"), None, None),
            P(("row", "col"), None, None, None),
        ),
        out_specs=P(("row", "col"), None, None),
        check_vma=False,
    )
```

```python
import functools

import jax
import jax.numpy as jnp
from jax import lax
from jax.experimental import pallas as pl
from jax.experimental.pallas import tpu as pltpu
from jax.sharding import PartitionSpec as P

MESH = pl.DeviceIdType.MESH
BF = jnp.bfloat16
F32 = jnp.float32
SOFTEN = 0.0025
GAIN = 256.0

NR, NC = 16, 8
CL, R, PS, K, FAR, NP = 16, 16, 512, 32, 32, 64
CHUNK = 64
NEIGHBOURS = [(0, -1), (0, 1), (-1, -1), (-1, 0), (-1, 1), (1, -1), (1, 0), (1, 1)]


def inside(row, col):
    rows = jnp.logical_and(row >= 0, row < NR)
    return jnp.logical_and(rows, jnp.logical_and(col >= 0, col < NC))


def pair_ids(pairs, s):
    a = pairs[0, s]
    b = pairs[1, s]
    b = jnp.where(b < 0, 4 * CL + a, b)
    o = lax.shift_right_logical(b, 4)
    l = lax.bitwise_and(b, CL - 1)
    down = lax.shift_right_logical(o * 11, 5)
    wr = jnp.clip(1 - CL + down * CL + l, 0, CL + 1)
    return a, o - 3 * down, wr


def make_tile(s, tile, pairs, tables, wc_ref, row0, col0):
    a, wc, wr = pair_ids(pairs, s)
    x0 = (row0 * CL + a).astype(F32) + 0.5
    y0 = col0.astype(F32) + 0.5
    at = pl.ds(wr + 7, 1)
    bx = wc_ref[wc, 0, at, :] - x0
    by = wc_ref[wc, 1, at, :] - y0
    bz = wc_ref[wc, 2, at, :]
    nb = GAIN * (bx * bx + by * by + bz * bz + SOFTEN)
    bx, by, bz = (-2.0 * GAIN) * bx, (-2.0 * GAIN) * by, (-2.0 * GAIN) * bz
    bx, by, bz, nb = [jnp.broadcast_to(v, (8, PS)) for v in (bx, by, bz, nb)]
    for p in range(0, PS, 16):
        for q in range(0, PS, 128):
            ql = slice(q, q + 128)
            halves = []
            for h in (p, p + 8):
                ax, ay, az, na = [tables[a, i, h : h + 8, :] for i in range(4)]
                sq = (na + nb[:, ql]) + ax * bx[:, ql]
                sq = sq + (ay * by[:, ql] + az * bz[:, ql])
                halves.append(lax.rsqrt(sq))
            tile[p : p + 16, ql] = jnp.concatenate(halves, axis=0).astype(BF)


def use_tile(s, tile, pairs, wr_ref, f_ref, b_ref):
    a, wc, wr = pair_ids(pairs, s)
    left = wr_ref[1, a + 1]
    right = wr_ref[wc, wr]
    t = tile[...]
    rows = pl.ds(pl.multiple_of(s * R, R), R)
    f_ref[rows, :] = lax.dot_general(
        right, t, (((1,), (1,)), ((), ())), preferred_element_type=F32
    ).astype(BF)
    b_ref[rows, :] = jnp.dot(left, t, preferred_element_type=F32).astype(BF)


def one_hot(codes, first, count):
    rows = lax.broadcasted_iota(jnp.int32, (count, NP * R), 0) + first
    return jnp.where(rows == codes, 1.0, 0.0).astype(BF)


def slot_codes(pairs_v):
    a = pairs_v[0:1, :]
    b = pairs_v[1:2, :]
    alive = b >= 0
    b = jnp.maximum(b, 0)
    o = lax.shift_right_logical(b, 4)
    l = lax.bitwise_and(b, 15)
    down = jnp.where(o >= 6, 2, jnp.where(o >= 3, 1, 0))
    wc = o - 3 * down
    wr = (down - 1) * CL + l + 1
    same = jnp.logical_and(o == 4, l == a)
    fwd = jnp.where(alive, a, -1)
    bwd = jnp.where(jnp.logical_and(alive, jnp.logical_not(same)), wc * (CL + 2) + wr, -1)
    slot = lax.broadcasted_iota(jnp.int32, (NP, NP * R), 0)
    lane = lax.broadcasted_iota(jnp.int32, (NP, NP * R), 1)
    spread = jnp.where(lax.shift_right_logical(lane, 4) == slot, 1.0, 0.0).astype(BF)
    inner = lax.bitwise_and(lax.broadcasted_iota(jnp.int32, (1, NP * R), 1), 15)
    out = []
    for v in (fwd, bwd):
        v = jnp.broadcast_to(v, (8, NP)).astype(F32).astype(BF)
        v = jnp.dot(v, spread, preferred_element_type=F32)[0:1, :]
        out.append(v.astype(jnp.int32) * R + inner)
    return out


def body(
    pairs_h, far_h, coords, rhs, basis, coupling, out,
    pairs, far, pairs_v, own_c, wc_ref, wr_ref, bas, cpl, tables, every, tile0, tile1, f_ref, b_ref, hot_f, hot_b, picked,
    send, back_c, back_r,
    loc_sem, hs_sem, hr_sem, g1s, g1r, g2s, g2r, g3s, g3r, bs_sem, br_sem,
):
    row = lax.axis_index("row")
    col = lax.axis_index("col")
    core = lax.rem(col, 2)
    cy = col // 2

    loads = [
        pltpu.make_async_copy(coords, own_c, loc_sem.at[0]),
        pltpu.make_async_copy(rhs, wr_ref.at[1, pl.ds(1, CL)], loc_sem.at[1]),
        pltpu.make_async_copy(basis, bas, loc_sem.at[2]),
        pltpu.make_async_copy(coupling, cpl, loc_sem.at[3]),
        pltpu.make_async_copy(coords, wc_ref.at[1, :, pl.ds(8, CL)], loc_sem.at[4]),
        pltpu.make_async_copy(pairs_h, pairs, loc_sem.at[5]),
        pltpu.make_async_copy(far_h, far, loc_sem.at[6]),
        pltpu.make_async_copy(pairs_h, pairs_v, loc_sem.at[7]),
    ]

    barrier = pltpu.get_barrier_semaphore()
    x, z = lax.rem(row, 4), row // 4
    y_peers = [(row, lax.rem(col + 2 * k, NC)) for k in (1, 2, 3)]
    x_peers = [(z * 4 + lax.rem(x + k, 4), col) for k in (1, 2, 3)]
    z_peers = [(lax.rem(z + k, 4) * 4 + x, col) for k in (1, 2, 3)]
    count = jnp.int32(9)
    for dr, dc in NEIGHBOURS:
        there = inside(row + dr, col + dc)
        count = count + there.astype(jnp.int32)

        @pl.when(there)
        def _():
            pl.semaphore_signal(
                barrier, inc=1, device_id=(row + dr, col + dc), device_id_type=MESH
            )

    for target in y_peers + x_peers + z_peers:
        pl.semaphore_signal(barrier, inc=1, device_id=target, device_id_type=MESH)
    for i in (0, 1, 2, 4, 5, 6, 7):
        loads[i].start()

    pl.semaphore_wait(barrier, count)

    def remote(src, dst, s, r, target):
        return pltpu.make_async_remote_copy(
            src_ref=src, dst_ref=dst, send_sem=s, recv_sem=r, device_id=target, device_id_type=MESH
        )

    def lend(k, dr, dc, i):
        if dr == 0:
            own, near = pl.ds(0, CL), pl.ds(1, CL)
        elif dr > 0:
            own, near = pl.ds(CL - 1, 1), pl.ds(0, 1)
        else:
            own, near = pl.ds(0, 1), pl.ds(CL + 1, 1)
        if i == 0:
            at = pl.ds(near.start + 7, near.size)
            src, dst = coords.at[:, own], wc_ref.at[1 - dc, :, at]
        else:
            src, dst = rhs.at[own], wr_ref.at[1 - dc, near]
        return remote(src, dst, hs_sem.at[k, i], hr_sem.at[k, i], (row + dr, col + dc))

    slow, fast = 2 * core - 1, 1 - 2 * core
    for i in range(2):
        pl.when(inside(row, col + slow))(lend(core, 0, slow, i).start)
        for k, (dr, dc) in list(enumerate(NEIGHBOURS))[2:]:
            pl.when(inside(row + dr, col + dc))(lend(k, dr, dc, i).start)
        pl.when(inside(row, col + fast))(lend(1 - core, 0, fast, i).start)
    loads[3].start()

    loads[1].wait()
    loads[2].wait()
    lane_of = lax.shift_right_logical(lax.broadcasted_iota(jnp.int32, (R, 4 * K), 1), 5)
    for j in range(CL // 4):
        left = wr_ref[1, 1 + 4 * j : 5 + 4 * j].reshape(4 * R, PS)
        right = bas[4 * j : 4 * j + 4].reshape(4 * K, PS)
        full = lax.dot_general(left, right, (((1,), (1,)), ((), ())), preferred_element_type=F32)
        mine = jnp.zeros((R, 4 * K), F32)
        for i in range(4):
            mine = mine + jnp.where(lane_of == i, full[i * R : (i + 1) * R, :], 0.0)
        every[row * (NC // 2) + cy, core * 4 + j] = mine.astype(BF)

    first = []
    for k in (1, 2, 3):
        ref = every.at[row * (NC // 2) + cy, pl.ds(core * 4, 4)]
        first.append(remote(ref, ref, g1s.at[k - 1], g1r.at[k - 1], y_peers[k - 1]))
    for c in first:
        c.start()

    loads[0].wait()
    steps = lax.broadcasted_iota(jnp.int32, (CL, PS), 0) + row * CL
    ox = own_c[0] - (steps.astype(F32) + 0.5)
    oy = own_c[1] - (col.astype(F32) + 0.5)
    oz = own_c[2]
    on = GAIN * (ox * ox + oy * oy + oz * oz)
    for i, v in enumerate((ox, oy, oz, on)):
        v = v.T
        for g in range(CL):
            tables[g, i] = jnp.broadcast_to(v[:, g : g + 1], (PS, 128))

    loads[7].wait()
    fwd, bwd = slot_codes(pairs_v[...])
    hot_f[...] = one_hot(fwd, 0, CL * R)
    wide = (CL + 2) * R
    for i in range(3):
        hot_b[i * wide : (i + 1) * wide, :] = one_hot(bwd, i * wide, wide)

    loads[4].wait()
    loads[5].wait()
    tiles = (tile0, tile1)
    build = functools.partial(
        make_tile, pairs=pairs, tables=tables, wc_ref=wc_ref, row0=row, col0=col
    )
    use = functools.partial(use_tile, pairs=pairs, wr_ref=wr_ref, f_ref=f_ref, b_ref=b_ref)

    def sweep(lo, hi):
        @pl.loop(lo, hi)
        def _(i):
            for j in range(2):

                @pl.when(i < NP + j)
                def _():
                    s = 2 * i + j
                    use(s, tiles[j])
                    build(s + 1, tiles[1 - j])

    def settle(copies):
        for (dr, dc), c in zip(NEIGHBOURS, copies):
            pl.when(inside(row + dr, col + dc))(c.wait_send)
            pl.when(inside(row - dr, col - dc))(c.wait_recv)

    settle([lend(k, dr, dc, 0) for k, (dr, dc) in enumerate(NEIGHBOURS)])
    build(0, tile0)
    settle([lend(k, dr, dc, 1) for k, (dr, dc) in enumerate(NEIGHBOURS)])
    sweep(0, 2)
    for c in first:
        c.wait()
    def blend(zero, one):
        return zero * (1 - core) + one * core

    second = []
    ref = every.at[pl.ds(row * 4, 4), pl.ds(core * 4, 4)]
    for k in range(3):
        target = (blend(x_peers[k][0], z_peers[k][0]), col)
        second.append(remote(ref, ref, g2s.at[k], g2r.at[k], target))
    for c in second:
        c.start()
    sweep(2, 6)
    for c in second:
        c.wait()
    second = []
    for m in range(4):
        at = blend(z * 16 + m * 4, m * 16 + x * 4)
        ref = every.at[pl.ds(at, 4), pl.ds(core * 4, 4)]
        for k in range(3):
            target = (blend(z_peers[k][0], x_peers[k][0]), col)
            n = 3 + 3 * m + k
            second.append(remote(ref, ref, g2s.at[n], g2r.at[n], target))
    for c in second:
        c.start()
    sweep(6, 28)
    for c in second:
        c.wait()
    ref = every.at[:, pl.ds(core * 4, 4)]
    third = remote(ref, ref, g3s.at[0], g3r.at[0], (row, col + 1 - 2 * core))
    third.start()
    sweep(28, NP // 2 - 1)
    use(NP - 2, tile0)
    build(NP - 1, tile1)
    use(NP - 1, tile1)

    terms = b_ref[...]

    def owed(k, dr, dc):
        if dr == 0:
            src, dst = send.at[dc + 1, pl.ds(1, CL)], back_c.at[k]
        else:
            src = send.at[dc + 1, pl.ds(0 if dr < 0 else CL + 1, 1)]
            dst = back_r.at[pl.ds(k - 2, 1)]
        return remote(src, dst, bs_sem.at[k], br_sem.at[k], (row + dr, col + dc))

    def give(k, dr, dc):
        pl.when(inside(row + dr, col + dc))(owed(k, dr, dc).start)

    for side in (core, 1 - core):
        dc = 2 * side - 1
        part = jnp.dot(hot_b[pl.ds(pl.multiple_of((dc + 1) * wide, R), wide), :], terms, preferred_element_type=F32)
        send[dc + 1] = part.astype(BF).reshape(CL + 2, R, PS)
        give(side, 0, dc)
        give(2 + 2 * side, -1, dc)
        give(5 + 2 * side, 1, dc)
    for at, k, dr in ((0, 3, -1), (CL + 1, 6, 1)):
        part = jnp.dot(hot_b[wide + at * R : wide + (at + 1) * R, :], terms, preferred_element_type=F32)
        send[1, at] = part.astype(BF)
        give(k, dr, 0)
    near = jnp.dot(hot_b[wide + R : wide + R + CL * R, :], terms, preferred_element_type=F32)
    near = near + jnp.dot(hot_f[...], f_ref[...], preferred_element_type=F32)
    out[...] = near.reshape(CL, R, PS)

    third.wait()
    loads[3].wait()
    loads[6].wait()

    @pl.loop(0, CL, unroll=4)
    def _(g):
        for f in range(0, FAR, 4):
            mine = jnp.zeros((R, 4 * K), F32)
            for j in range(4):
                h = far[g, f + j]
                at = lax.bitwise_and(lax.shift_right_logical(h, 2), 7)
                got = every[lax.shift_right_logical(h, 5), at].astype(F32)
                got = pltpu.roll(got, lax.bitwise_and(j - h, 3) * K, 1)
                mine = jnp.where(lane_of == j, got, mine)
            picked[g, :, f * K : (f + 4) * K] = mine.astype(BF)

    inner = [jnp.dot(picked[g], cpl[g], preferred_element_type=F32).astype(BF) for g in range(CL)]
    for g in range(CL):
        out[g] += jnp.dot(inner[g], bas[g], preferred_element_type=F32)

    settle([owed(k, dr, dc) for k, (dr, dc) in enumerate(NEIGHBOURS)])
    for k, (dr, dc) in enumerate(NEIGHBOURS):

        @pl.when(inside(row - dr, col - dc))
        def _():
            if dr == 0:
                out[...] += back_c[k].astype(F32)
            else:
                at = CL - 1 if dr < 0 else 0
                out[at] += back_r[k - 2].astype(F32)


def per_device(coords, rhs, near_pairs, far_list, basis, coupling):
    vmem = pl.BlockSpec(memory_space=pltpu.VMEM)
    hbm = pl.BlockSpec(memory_space=pltpu.HBM)
    dma = pltpu.SemaphoreType.DMA
    def hold(x):
        return pltpu.with_memory_space_constraint(x, pltpu.HBM)

    return pl.pallas_call(
        body,
        out_shape=pltpu.VMEM((CL, R, PS), F32),
        in_specs=[hbm] * 6,
        out_specs=vmem,
        scratch_shapes=[
            pltpu.SMEM((2, NP), jnp.int32),
            pltpu.SMEM((CL, FAR), jnp.int32),
            pltpu.VMEM((2, NP), jnp.int32),
            pltpu.VMEM((3, CL, PS), F32),
            pltpu.VMEM((3, 3, CL + 16, PS), F32),
            pltpu.VMEM((3, CL + 2, R, PS), BF),
            pltpu.VMEM((CL, K, PS), BF),
            pltpu.VMEM((CL, FAR * K, K), BF),
            pltpu.VMEM((CL, 4, PS, 128), F32),
            pltpu.VMEM((NR * NC // 2, 2 * CL // 4, R, 4 * K), BF),
            pltpu.VMEM((PS, PS), BF),
            pltpu.VMEM((PS, PS), BF),
            pltpu.VMEM((NP * R, PS), BF),
            pltpu.VMEM((NP * R, PS), BF),
            pltpu.VMEM((CL * R, NP * R), BF),
            pltpu.VMEM((3 * (CL + 2) * R, NP * R), BF),
            pltpu.VMEM((CL, R, FAR * K), BF),
            pltpu.VMEM((3, CL + 2, R, PS), BF),
            pltpu.VMEM((2, CL, R, PS), BF),
            pltpu.VMEM((6, R, PS), BF),
            dma((8,)),
            dma((8, 2)),
            dma((8, 2)),
            dma((3,)),
            dma((3,)),
            dma((15,)),
            dma((15,)),
            dma((1,)),
            dma((1,)),
            dma((8,)),
            dma((8,)),
        ],
        compiler_params=pltpu.CompilerParams(
            collective_id=0, has_side_effects=True, vmem_limit_bytes=62 * 2**20
        ),
        name="hmatrix",
    )(
        hold(near_pairs.T),
        hold(far_list),
        hold(coords.transpose(1, 0, 2)),
        hold(rhs),
        hold(basis),
        hold(coupling.reshape(CL, FAR * K, K)),
    )


def solution(mesh):
    return jax.shard_map(
        per_device,
        mesh=mesh,
        in_specs=(
            P(("row", "col"), None, None),
            P(("row", "col"), None, None),
            P(("row", "col"), None),
            P(("row", "col"), None),
            P(("row", "col"), None, None),
            P(("row", "col"), None, None, None),
        ),
        out_specs=P(("row", "col"), None, None),
        check_vma=False,
    )
```

```python
import functools

import jax
import jax.numpy as jnp
from jax import lax
from jax.experimental import pallas as pl
from jax.experimental.pallas import tpu as pltpu
from jax.sharding import PartitionSpec as P

MESH = pl.DeviceIdType.MESH
BF = jnp.bfloat16
F32 = jnp.float32
SOFTEN = 0.0025
GAIN = 256.0

NR, NC = 16, 8
CL, R, PS, K, FAR, NP = 16, 16, 512, 32, 32, 64
CHUNK = 64
NEIGHBOURS = [(0, -1), (0, 1), (-1, -1), (-1, 0), (-1, 1), (1, -1), (1, 0), (1, 1)]


def inside(row, col):
    rows = jnp.logical_and(row >= 0, row < NR)
    return jnp.logical_and(rows, jnp.logical_and(col >= 0, col < NC))


def pair_ids(pairs, s):
    a = pairs[0, s]
    b = pairs[1, s]
    b = jnp.where(b < 0, 4 * CL + a, b)
    o = lax.shift_right_logical(b, 4)
    l = lax.bitwise_and(b, CL - 1)
    down = lax.shift_right_logical(o * 11, 5)
    wr = jnp.clip(1 - CL + down * CL + l, 0, CL + 1)
    return a, o - 3 * down, wr


def make_tile(s, tile, pairs, tables, wc_ref, row0, col0):
    a, wc, wr = pair_ids(pairs, s)
    x0 = (row0 * CL + a).astype(F32) + 0.5
    y0 = col0.astype(F32) + 0.5
    at = pl.ds(wr + 7, 1)
    bx = wc_ref[wc, 0, at, :] - x0
    by = wc_ref[wc, 1, at, :] - y0
    bz = wc_ref[wc, 2, at, :]
    nb = GAIN * (bx * bx + by * by + bz * bz + SOFTEN)
    bx, by, bz = (-2.0 * GAIN) * bx, (-2.0 * GAIN) * by, (-2.0 * GAIN) * bz
    bx, by, bz, nb = [jnp.broadcast_to(v, (8, PS)) for v in (bx, by, bz, nb)]
    for p in range(0, PS, 16):
        for q in range(0, PS, 128):
            ql = slice(q, q + 128)
            halves = []
            for h in (p, p + 8):
                ax, ay, az, na = [tables[a, i, h : h + 8, :] for i in range(4)]
                sq = (na + nb[:, ql]) + ax * bx[:, ql]
                sq = sq + (ay * by[:, ql] + az * bz[:, ql])
                halves.append(lax.rsqrt(sq))
            tile[p : p + 16, ql] = jnp.concatenate(halves, axis=0).astype(BF)


def use_tile(s, tile, pairs, wr_ref, f_ref, b_ref):
    a, wc, wr = pair_ids(pairs, s)
    left = wr_ref[1, a + 1]
    right = wr_ref[wc, wr]
    t = tile[...]
    rows = pl.ds(pl.multiple_of(s * R, R), R)
    f_ref[rows, :] = lax.dot_general(
        right, t, (((1,), (1,)), ((), ())), preferred_element_type=F32
    ).astype(BF)
    b_ref[rows, :] = jnp.dot(left, t, preferred_element_type=F32).astype(BF)


def one_hot(codes, first, count):
    rows = lax.broadcasted_iota(jnp.int32, (count, NP * R), 0) + first
    return jnp.where(rows == codes, 1.0, 0.0).astype(BF)


def slot_codes(pairs_v):
    a = pairs_v[0:1, :]
    b = pairs_v[1:2, :]
    alive = b >= 0
    b = jnp.maximum(b, 0)
    o = lax.shift_right_logical(b, 4)
    l = lax.bitwise_and(b, 15)
    down = jnp.where(o >= 6, 2, jnp.where(o >= 3, 1, 0))
    wc = o - 3 * down
    wr = (down - 1) * CL + l + 1
    same = jnp.logical_and(o == 4, l == a)
    fwd = jnp.where(alive, a, -1)
    bwd = jnp.where(jnp.logical_and(alive, jnp.logical_not(same)), wc * (CL + 2) + wr, -1)
    slot = lax.broadcasted_iota(jnp.int32, (NP, NP * R), 0)
    lane = lax.broadcasted_iota(jnp.int32, (NP, NP * R), 1)
    spread = jnp.where(lax.shift_right_logical(lane, 4) == slot, 1.0, 0.0).astype(BF)
    inner = lax.bitwise_and(lax.broadcasted_iota(jnp.int32, (1, NP * R), 1), 15)
    out = []
    for v in (fwd, bwd):
        v = jnp.broadcast_to(v, (8, NP)).astype(F32).astype(BF)
        v = jnp.dot(v, spread, preferred_element_type=F32)[0:1, :]
        out.append(v.astype(jnp.int32) * R + inner)
    return out


def body(
    pairs_h, far_h, coords, rhs, basis, coupling, out,
    pairs, far, pairs_v, own_c, wc_ref, wr_ref, bas, cpl, tables, every, tile0, tile1, f_ref, b_ref, hot_f, hot_b, picked,
    send, back_c, back_r,
    loc_sem, hs_sem, hr_sem, g1s, g1r, g2s, g2r, g3s, g3r, bs_sem, br_sem,
):
    row = lax.axis_index("row")
    col = lax.axis_index("col")
    core = lax.rem(col, 2)
    cy = col // 2

    loads = [
        pltpu.make_async_copy(coords, own_c, loc_sem.at[0]),
        pltpu.make_async_copy(rhs, wr_ref.at[1, pl.ds(1, CL)], loc_sem.at[1]),
        pltpu.make_async_copy(basis, bas, loc_sem.at[2]),
        pltpu.make_async_copy(coupling, cpl, loc_sem.at[3]),
        pltpu.make_async_copy(coords, wc_ref.at[1, :, pl.ds(8, CL)], loc_sem.at[4]),
        pltpu.make_async_copy(pairs_h, pairs, loc_sem.at[5]),
        pltpu.make_async_copy(far_h, far, loc_sem.at[6]),
        pltpu.make_async_copy(pairs_h, pairs_v, loc_sem.at[7]),
    ]

    barrier = pltpu.get_barrier_semaphore()
    x, z = lax.rem(row, 4), row // 4
    y_peers = [(row, lax.rem(col + 2 * k, NC)) for k in (1, 2, 3)]
    x_peers = [(z * 4 + lax.rem(x + k, 4), col) for k in (1, 2, 3)]
    z_peers = [(lax.rem(z + k, 4) * 4 + x, col) for k in (1, 2, 3)]
    count = jnp.int32(9)
    for dr, dc in NEIGHBOURS:
        there = inside(row + dr, col + dc)
        count = count + there.astype(jnp.int32)

        @pl.when(there)
        def _():
            pl.semaphore_signal(
                barrier, inc=1, device_id=(row + dr, col + dc), device_id_type=MESH
            )

    for target in y_peers + x_peers + z_peers:
        pl.semaphore_signal(barrier, inc=1, device_id=target, device_id_type=MESH)
    for i in (0, 1, 2, 4, 5, 6, 7):
        loads[i].start()

    pl.semaphore_wait(barrier, count)

    def remote(src, dst, s, r, target):
        return pltpu.make_async_remote_copy(
            src_ref=src, dst_ref=dst, send_sem=s, recv_sem=r, device_id=target, device_id_type=MESH
        )

    def lend(k, dr, dc, i):
        if dr == 0:
            own, near = pl.ds(0, CL), pl.ds(1, CL)
        elif dr > 0:
            own, near = pl.ds(CL - 1, 1), pl.ds(0, 1)
        else:
            own, near = pl.ds(0, 1), pl.ds(CL + 1, 1)
        if i == 0:
            at = pl.ds(near.start + 7, near.size)
            src, dst = coords.at[:, own], wc_ref.at[1 - dc, :, at]
        else:
            src, dst = rhs.at[own], wr_ref.at[1 - dc, near]
        return remote(src, dst, hs_sem.at[k, i], hr_sem.at[k, i], (row + dr, col + dc))

    slow, fast = 2 * core - 1, 1 - 2 * core
    for i in range(2):
        pl.when(inside(row, col + slow))(lend(core, 0, slow, i).start)
        for k, (dr, dc) in list(enumerate(NEIGHBOURS))[2:]:
            pl.when(inside(row + dr, col + dc))(lend(k, dr, dc, i).start)
        pl.when(inside(row, col + fast))(lend(1 - core, 0, fast, i).start)
    loads[3].start()

    loads[1].wait()
    loads[2].wait()
    lane_of = lax.shift_right_logical(lax.broadcasted_iota(jnp.int32, (R, 4 * K), 1), 5)
    for j in range(CL // 4):
        left = wr_ref[1, 1 + 4 * j : 5 + 4 * j].reshape(4 * R, PS)
        right = bas[4 * j : 4 * j + 4].reshape(4 * K, PS)
        full = lax.dot_general(left, right, (((1,), (1,)), ((), ())), preferred_element_type=F32)
        mine = jnp.zeros((R, 4 * K), F32)
        for i in range(4):
            mine = mine + jnp.where(lane_of == i, full[i * R : (i + 1) * R, :], 0.0)
        every[row * (NC // 2) + cy, core * 4 + j] = mine.astype(BF)

    first = []
    for k in (1, 2, 3):
        ref = every.at[row * (NC // 2) + cy, pl.ds(core * 4, 4)]
        first.append(remote(ref, ref, g1s.at[k - 1], g1r.at[k - 1], y_peers[k - 1]))
    for c in first:
        c.start()

    loads[0].wait()
    steps = lax.broadcasted_iota(jnp.int32, (CL, PS), 0) + row * CL
    ox = own_c[0] - (steps.astype(F32) + 0.5)
    oy = own_c[1] - (col.astype(F32) + 0.5)
    oz = own_c[2]
    on = GAIN * (ox * ox + oy * oy + oz * oz)
    for i, v in enumerate((ox, oy, oz, on)):
        v = v.T
        for g in range(CL):
            tables[g, i] = jnp.broadcast_to(v[:, g : g + 1], (PS, 128))

    loads[7].wait()
    fwd, bwd = slot_codes(pairs_v[...])
    hot_f[...] = one_hot(fwd, 0, CL * R)
    wide = (CL + 2) * R
    for i in range(3):
        hot_b[i * wide : (i + 1) * wide, :] = one_hot(bwd, i * wide, wide)

    loads[4].wait()
    loads[5].wait()
    tiles = (tile0, tile1)
    build = functools.partial(
        make_tile, pairs=pairs, tables=tables, wc_ref=wc_ref, row0=row, col0=col
    )
    use = functools.partial(use_tile, pairs=pairs, wr_ref=wr_ref, f_ref=f_ref, b_ref=b_ref)

    def sweep(lo, hi):
        @pl.loop(lo, hi)
        def _(i):
            for j in range(2):

                @pl.when(i < NP + j)
                def _():
                    s = 2 * i + j
                    use(s, tiles[j])
                    build(s + 1, tiles[1 - j])

    def settle(copies):
        for (dr, dc), c in zip(NEIGHBOURS, copies):
            pl.when(inside(row + dr, col + dc))(c.wait_send)
            pl.when(inside(row - dr, col - dc))(c.wait_recv)

    settle([lend(k, dr, dc, 0) for k, (dr, dc) in enumerate(NEIGHBOURS)])
    build(0, tile0)
    settle([lend(k, dr, dc, 1) for k, (dr, dc) in enumerate(NEIGHBOURS)])
    sweep(0, 4)
    for c in first:
        c.wait()
    def blend(zero, one):
        return zero * (1 - core) + one * core

    second = []
    ref = every.at[pl.ds(row * 4, 4), pl.ds(core * 4, 4)]
    for k in range(3):
        target = (blend(x_peers[k][0], z_peers[k][0]), col)
        second.append(remote(ref, ref, g2s.at[k], g2r.at[k], target))
    for c in second:
        c.start()
    sweep(4, 10)
    for c in second:
        c.wait()
    second = []
    for m in range(4):
        at = blend(z * 16 + m * 4, m * 16 + x * 4)
        ref = every.at[pl.ds(at, 4), pl.ds(core * 4, 4)]
        for k in range(3):
            target = (blend(z_peers[k][0], x_peers[k][0]), col)
            n = 3 + 3 * m + k
            second.append(remote(ref, ref, g2s.at[n], g2r.at[n], target))
    for c in second:
        c.start()
    sweep(10, 30)
    for c in second:
        c.wait()
    ref = every.at[:, pl.ds(core * 4, 4)]
    third = remote(ref, ref, g3s.at[0], g3r.at[0], (row, col + 1 - 2 * core))
    third.start()
    sweep(30, NP // 2 - 1)
    use(NP - 2, tile0)
    build(NP - 1, tile1)
    use(NP - 1, tile1)

    terms = b_ref[...]

    def owed(k, dr, dc):
        if dr == 0:
            src, dst = send.at[dc + 1, pl.ds(1, CL)], back_c.at[k]
        else:
            src = send.at[dc + 1, pl.ds(0 if dr < 0 else CL + 1, 1)]
            dst = back_r.at[pl.ds(k - 2, 1)]
        return remote(src, dst, bs_sem.at[k], br_sem.at[k], (row + dr, col + dc))

    def give(k, dr, dc):
        pl.when(inside(row + dr, col + dc))(owed(k, dr, dc).start)

    for side in (core, 1 - core):
        dc = 2 * side - 1
        part = jnp.dot(hot_b[pl.ds(pl.multiple_of((dc + 1) * wide, R), wide), :], terms, preferred_element_type=F32)
        send[dc + 1] = part.astype(BF).reshape(CL + 2, R, PS)
        give(side, 0, dc)
        give(2 + 2 * side, -1, dc)
        give(5 + 2 * side, 1, dc)
    for at, k, dr in ((0, 3, -1), (CL + 1, 6, 1)):
        part = jnp.dot(hot_b[wide + at * R : wide + (at + 1) * R, :], terms, preferred_element_type=F32)
        send[1, at] = part.astype(BF)
        give(k, dr, 0)
    near = jnp.dot(hot_b[wide + R : wide + R + CL * R, :], terms, preferred_element_type=F32)
    near = near + jnp.dot(hot_f[...], f_ref[...], preferred_element_type=F32)
    out[...] = near.reshape(CL, R, PS)

    third.wait()
    loads[3].wait()
    loads[6].wait()

    @pl.loop(0, CL, unroll=4)
    def _(g):
        for f in range(0, FAR, 4):
            mine = jnp.zeros((R, 4 * K), F32)
            for j in range(4):
                h = far[g, f + j]
                at = lax.bitwise_and(lax.shift_right_logical(h, 2), 7)
                got = every[lax.shift_right_logical(h, 5), at].astype(F32)
                got = pltpu.roll(got, lax.bitwise_and(j - h, 3) * K, 1)
                mine = jnp.where(lane_of == j, got, mine)
            picked[g, :, f * K : (f + 4) * K] = mine.astype(BF)

    inner = [jnp.dot(picked[g], cpl[g], preferred_element_type=F32).astype(BF) for g in range(CL)]
    for g in range(CL):
        out[g] += jnp.dot(inner[g], bas[g], preferred_element_type=F32)

    settle([owed(k, dr, dc) for k, (dr, dc) in enumerate(NEIGHBOURS)])
    for k, (dr, dc) in enumerate(NEIGHBOURS):

        @pl.when(inside(row - dr, col - dc))
        def _():
            if dr == 0:
                out[...] += back_c[k].astype(F32)
            else:
                at = CL - 1 if dr < 0 else 0
                out[at] += back_r[k - 2].astype(F32)


def per_device(coords, rhs, near_pairs, far_list, basis, coupling):
    vmem = pl.BlockSpec(memory_space=pltpu.VMEM)
    hbm = pl.BlockSpec(memory_space=pltpu.HBM)
    dma = pltpu.SemaphoreType.DMA
    def hold(x):
        return pltpu.with_memory_space_constraint(x, pltpu.HBM)

    return pl.pallas_call(
        body,
        out_shape=pltpu.VMEM((CL, R, PS), F32),
        in_specs=[hbm] * 6,
        out_specs=vmem,
        scratch_shapes=[
            pltpu.SMEM((2, NP), jnp.int32),
            pltpu.SMEM((CL, FAR), jnp.int32),
            pltpu.VMEM((2, NP), jnp.int32),
            pltpu.VMEM((3, CL, PS), F32),
            pltpu.VMEM((3, 3, CL + 16, PS), F32),
            pltpu.VMEM((3, CL + 2, R, PS), BF),
            pltpu.VMEM((CL, K, PS), BF),
            pltpu.VMEM((CL, FAR * K, K), BF),
            pltpu.VMEM((CL, 4, PS, 128), F32),
            pltpu.VMEM((NR * NC // 2, 2 * CL // 4, R, 4 * K), BF),
            pltpu.VMEM((PS, PS), BF),
            pltpu.VMEM((PS, PS), BF),
            pltpu.VMEM((NP * R, PS), BF),
            pltpu.VMEM((NP * R, PS), BF),
            pltpu.VMEM((CL * R, NP * R), BF),
            pltpu.VMEM((3 * (CL + 2) * R, NP * R), BF),
            pltpu.VMEM((CL, R, FAR * K), BF),
            pltpu.VMEM((3, CL + 2, R, PS), BF),
            pltpu.VMEM((2, CL, R, PS), BF),
            pltpu.VMEM((6, R, PS), BF),
            dma((8,)),
            dma((8, 2)),
            dma((8, 2)),
            dma((3,)),
            dma((3,)),
            dma((15,)),
            dma((15,)),
            dma((1,)),
            dma((1,)),
            dma((8,)),
            dma((8,)),
        ],
        compiler_params=pltpu.CompilerParams(
            collective_id=0, has_side_effects=True, vmem_limit_bytes=62 * 2**20
        ),
        name="hmatrix",
    )(
        hold(near_pairs.T),
        hold(far_list),
        hold(coords.transpose(1, 0, 2)),
        hold(rhs),
        hold(basis),
        hold(coupling.reshape(CL, FAR * K, K)),
    )


def solution(mesh):
    return jax.shard_map(
        per_device,
        mesh=mesh,
        in_specs=(
            P(("row", "col"), None, None),
            P(("row", "col"), None, None),
            P(("row", "col"), None),
            P(("row", "col"), None),
            P(("row", "col"), None, None),
            P(("row", "col"), None, None, None),
        ),
        out_specs=P(("row", "col"), None, None),
        check_vma=False,
    )
```
